1024 devices in a mesh: dp: 64 (over z, x), expert: 16 (over y, core).
Axes of the slice: x: 8, y: 8, z: 8, core: 2. Of those that a mesh axis runs over, the one named last changes fastest.
Arguments:
- d_out: bfloat16 [2, 131072, 2048], P(None, ('dp', 'expert')), may hold values from -6 to 6
- routes: int32 [2, 131072, 8], P(None, ('dp', 'expert')), may hold values from 0 to 127, as said below
- slots: int32 [2, 131072, 8], P(None, ('dp', 'expert')), may hold values from -1 to 15, as said below
- route_probs: bfloat16 [2, 131072, 8], P(None, ('dp', 'expert')), may hold values from 0.029907227 to 0.5
- token_counts: int32 [2, 1024], P(None, ('dp', 'expert')), may hold values from 42 to 128, as said below
- hidden: bfloat16 [2, 64, 256, 3072], P(None, 'dp', None, 'expert'), may hold values from -0.59765625 to 0.59765625
- w_down: bfloat16 [3072, 2048], P('expert'), may hold values from -0.21875 to 0.21875
Outputs:
- d_hidden: bfloat16 [2, 64, 256, 3072], P(None, 'dp', None, 'expert')
- d_w2: float32 [2048, 3072], P('dp', 'expert')
- d_probs: float32 [2, 131072, 8], P(None, ('dp', 'expert'))
The draws below stay inside these ranges and needn't reach their ends.
Inputs may be any that keep to these rules, and one draw needn't show every extreme that they name: `routes`: each row names 8 different experts. Only experts below 4 belong to the window; window expert e is held by indices 4 * e to 4 * e + 3 of the expert axis, each with its share of the hidden units in order. A slot is -1 exactly where the route names an expert at or above 4 or where the token's position in its device's block of 128 is at or past that device's count; the routes of one device to one window expert in one microbatch hold distinct slots. In every microbatch one window expert receives 16 rows from every device. `token_counts`: A device's valid tokens are the first ones of its block.
All inputs are finite; a program needn't handle non-finite values.
Results may differ from the reference program's by a relative error of at most 0.003.
Values may be sent and summed in bfloat16 or wider, within the bound.
A program may use at most 32 MiB of HBM per device.

```python
import math
import jax
import jax.numpy as jnp
from jax import lax

D = 2048
FF = 768
ALL_EXPERTS = 128
TOPK = 8
MB = 2
TOK_DEV = 128
CAP = 16
EXPERTS = 4
SOURCES = 1024
TOKENS = 131072
SLOTS = 256
N_DP = 64
N_EXPERT = 16


def counts_table(key):
    key_count = jax.random.fold_in(key, 11)
    key_shift = jax.random.fold_in(key, 13)
    lowest = TOK_DEV // 3
    device_pos = jnp.arange(SOURCES, dtype=jnp.int32)
    ramp = lowest + (TOK_DEV - lowest) * device_pos // max(SOURCES - 1, 1)
    jitter = jax.random.randint(key_count, (MB, SOURCES), 0, TOK_DEV // 16 + 1)
    common = jax.random.randint(key_shift, (MB, 1), 0, (TOK_DEV - lowest) // 2 + 1)
    interior = (device_pos > 0) & (device_pos < SOURCES - 1)
    return jnp.minimum(ramp[None, :] + jnp.where(interior[None, :], jitter + common, 0), TOK_DEV).astype(jnp.int32)


def plan_one(key_one, valid_count, busiest):
    key_list = jax.random.split(key_one, 5)
    draw_one = jax.random.randint(key_list[0], (EXPERTS,), 0, CAP + 1)
    second = jax.random.randint(key_list[1], (EXPERTS,), 0, CAP + 1)
    expert_index = jnp.arange(EXPERTS, dtype=jnp.int32)
    expert_load = jnp.where(expert_index == busiest, CAP, CAP - draw_one * second // (4 * CAP))
    expert_load = jnp.where(expert_index == 0, jnp.maximum(expert_load, 1), expert_load)
    row_index = jnp.arange(EXPERTS * CAP, dtype=jnp.int32)
    expert = row_index // CAP
    slot_rank = row_index % CAP
    filled = slot_rank < expert_load[expert]
    order_pos = jnp.cumsum(filled.astype(jnp.int32)) - 1
    tokens_local = jnp.arange(TOK_DEV, dtype=jnp.int32)
    shuffle_key = jax.random.permutation(key_list[2], TOK_DEV) + jnp.where(tokens_local >= valid_count, TOK_DEV, 0)
    shuffled = jnp.argsort(shuffle_key)
    safe_pos = jnp.maximum(order_pos, 0)
    target = jnp.where(filled, shuffled[safe_pos % valid_count], TOK_DEV)
    column = jnp.where(filled, safe_pos // valid_count, TOPK)
    window_ids = jnp.full((TOK_DEV, TOPK), -1, jnp.int32).at[target, column].set(expert, mode='drop')
    window_slots = jnp.full((TOK_DEV, TOPK), -1, jnp.int32).at[target, column].set(slot_rank, mode='drop')
    spare_range = ALL_EXPERTS - EXPERTS
    offset = jax.random.randint(key_list[3], (TOK_DEV, 1), 0, spare_range)
    offset = jnp.where(tokens_local[:, None] == 0, spare_range - TOPK, offset)
    spare_ids = EXPERTS + (offset + jnp.arange(TOPK, dtype=jnp.int32)[None, :]) % spare_range
    route_ids = jnp.where(window_ids >= 0, window_ids, spare_ids)
    rotation = jax.random.randint(key_list[4], (TOK_DEV, 1), 0, TOPK)
    columns = (jnp.arange(TOPK, dtype=jnp.int32)[None, :] + rotation) % TOPK
    return (jnp.take_along_axis(route_ids, columns, axis=1), jnp.take_along_axis(window_slots, columns, axis=1))


def route_plan(key):
    valid_table = counts_table(key)
    key_plan = jax.random.fold_in(key, 12)
    busiest = jax.random.randint(jax.random.fold_in(key_plan, 1), (MB,), 0, EXPERTS)
    key_list = jax.random.split(jax.random.fold_in(key_plan, 2), MB * SOURCES)
    busiest_all = jnp.repeat(busiest, SOURCES)
    route_ids, slot_ids = jax.vmap(plan_one)(key_list, valid_table.reshape(-1), busiest_all)
    return (route_ids.reshape(MB, TOKENS, TOPK).astype(jnp.int32), slot_ids.reshape(MB, TOKENS, TOPK).astype(jnp.int32))


def draw_token_counts(key, part):
    return counts_table(key)


def draw_routes(key, part):
    return route_plan(key)[0]


def draw_slots(key, part):
    return route_plan(key)[1]


def block_scale(own_key, shape, shards, smallest, largest):
    loudness, own = 1.0, jax.random.fold_in(own_key, 6)
    for position, blocks in shards:
        heights = jnp.exp(jax.random.uniform(jax.random.fold_in(own, position), (blocks,), jnp.float32, smallest / len(shards), largest / len(shards)))
        loudness = loudness * jnp.repeat(heights, shape[position] // blocks).reshape([-1 if axis == position else 1 for axis in range(len(shape))])
    return loudness


def centred(stream_key, dims, scale, most, cuts=(), kind=jnp.bfloat16):
    result = scale * jax.random.normal(stream_key, dims, jnp.float32)
    if cuts:
        result = result * block_scale(stream_key, dims, cuts, -0.22, 0.18)
    return jnp.clip(result, -most, most).astype(kind)


def setup_inputs(seed: int = 0) -> dict:
    splits = jax.random.split(jax.random.key(seed), 8)
    d_out = centred(splits[0], (MB, TOKENS, D), 1.0, 6.0, ((1, 1024),))
    routes = draw_routes(jax.random.fold_in(splits[7], 71), 0)
    slots = draw_slots(jax.random.fold_in(splits[7], 71), 0)
    route_probs = jnp.clip(jnp.exp(math.log(0.5) - 2.816508 * jax.random.uniform(splits[3], (MB, TOKENS, TOPK), jnp.float32) ** block_scale(splits[3], (MB, TOKENS, TOPK), ((1, 1024),), -0.2, 0.2)), 0.029907227, 0.5).astype(jnp.bfloat16)
    token_counts = draw_token_counts(jax.random.fold_in(splits[7], 71), 0)
    hidden = centred(splits[5], (MB, N_DP, SLOTS, EXPERTS * FF), 0.1, 0.59765625, ((1, 64), (3, 16)))
    w_down = centred(splits[6], (EXPERTS * FF, D), FF ** -0.5, 0.21875, ((0, 16),))
    return dict(d_out=d_out, routes=routes, slots=slots, route_probs=route_probs, token_counts=token_counts, hidden=hidden, w_down=w_down)


def reference(d_out, routes, slots, route_probs, token_counts, hidden, w_down):
    token_total = jnp.sum(token_counts.astype(jnp.float32))
    grad_scale = jnp.float32(MB * TOKENS) / token_total
    group_rows = TOK_DEV * N_EXPERT

    def by_group(array):
        return jnp.swapaxes(array.reshape((MB, N_DP, group_rows) + array.shape[2:]), 0, 1)

    hidden_split = jnp.transpose(hidden.reshape(MB, N_DP, SLOTS, EXPERTS, FF), (0, 1, 3, 2, 4))
    group_data = (by_group(d_out), by_group(routes), by_group(slots), by_group(route_probs), jnp.swapaxes(hidden_split, 0, 1))
    weight_wide = w_down.reshape(EXPERTS, FF, D).astype(jnp.float32)
    batch_index = jnp.arange(MB, dtype=jnp.int32)[:, None, None]
    source = (jnp.arange(group_rows, dtype=jnp.int32) // TOK_DEV)[None, :, None]

    def one_group(accumulated, members):
        grad_rows, route_ids, slot_ids, probs_rows, hidden_rows = members
        filled = slot_ids >= 0
        expert_at = jnp.where(filled, route_ids, EXPERTS).astype(jnp.int32)
        column_at = jnp.where(filled, source * CAP + slot_ids, SLOTS).astype(jnp.int32)
        routed = jnp.zeros((MB, EXPERTS, SLOTS, D), jnp.bfloat16).at[batch_index, expert_at, column_at].set(grad_rows[:, :, None, :], mode="drop")
        weights = jnp.zeros((MB, EXPERTS, SLOTS), jnp.bfloat16).at[batch_index, expert_at, column_at].set(probs_rows, mode="drop")
        back_grad = jnp.einsum("mesd,efd->mesf", routed.astype(jnp.float32), weight_wide)
        hidden_wide = hidden_rows.astype(jnp.float32)
        slot_grad = jnp.sum(hidden_wide * back_grad, axis=3)
        weight_col = weights.astype(jnp.float32)[..., None]
        grad_hidden = ((grad_scale * weight_col) * back_grad).astype(jnp.bfloat16)
        weighted = (weight_col * routed.astype(jnp.float32)).astype(jnp.bfloat16)
        accumulated = accumulated + jnp.einsum("mesf,mesd->efd", hidden_wide, weighted.astype(jnp.float32))
        flat_grad = slot_grad.reshape(MB, EXPERTS * SLOTS)
        lookup = jnp.where(filled, route_ids * SLOTS + source * CAP + slot_ids, 0).astype(jnp.int32).reshape(MB, -1)
        returned = jnp.take_along_axis(flat_grad, lookup, axis=1).reshape(filled.shape)
        grad_probs = jnp.where(filled, grad_scale * returned, jnp.float32(0.0))
        return accumulated, (grad_hidden, grad_probs)

    initial = jnp.zeros((EXPERTS, FF, D), jnp.float32)
    summed, (grad_hidden, grad_probs) = lax.scan(one_group, initial, group_data)
    grad_hidden = jnp.swapaxes(grad_hidden, 0, 1)
    d_hidden = jnp.transpose(grad_hidden, (0, 1, 3, 2, 4)).reshape(MB, N_DP, SLOTS, EXPERTS * FF)
    d_probs = jnp.swapaxes(grad_probs, 0, 1).reshape(MB, TOKENS, TOPK)
    d_w2 = jnp.transpose((grad_scale * summed).reshape(EXPERTS * FF, D))
    return d_hidden, d_w2, d_probs
```

```python
import functools
import math

import jax
import jax.numpy as jnp
from jax import lax
from jax.experimental import pallas as pl
from jax.experimental.pallas import tpu as pltpu
from jax.sharding import PartitionSpec as P

MESH = pl.DeviceIdType.MESH
F32 = jnp.float32
BF16 = jnp.bfloat16
RING = 8
GROUP = 4
AHEAD = 2


def iota(shape, dimension):
    return lax.broadcasted_iota(jnp.int32, shape, dimension)


def kernel(
    nz, nx, scale_top,
    dout_ref, routes_ref, slots_ref, probs_ref, counts_ref, hid_ref, w_ref,
    dh_ref, dw_ref, dp_ref,
    sel, out, outw, rows, roww, wmat, wrow, back, ht, xs, xr, zs, zr, cs, cxr, czr, rs, rr,
    near_s, near_r, mate_s, mate_r, sib_s, sib_r, x_s, x_r, z_s, z_r, c_s, c_r, ret_s, ret_r,
):
    d = lax.axis_index("dp")
    j = lax.axis_index("expert")
    z, x = lax.div(d, nx), lax.rem(d, nx)
    y, c = lax.div(j, 2), lax.rem(j, 2)
    sign = 2 * lax.rem(y, 2) - 1
    mine = lax.div(y, 2)
    batches, choose, toks = routes_ref.shape
    hidden = w_ref.shape[0]
    cap = out.shape[3]
    cw = out.shape[4]
    peers = 2 * RING
    window = peers // GROUP
    slot_rows = window * cap
    total_rows = batches * peers * cap

    def along_y(offset):
        return lax.rem(y + offset + 2 * RING, RING)

    mate_y = y - sign
    mate = (d, mate_y * 2 + c)
    sibling = (d, y * 2 + 1 - c)
    sources = [along_y(sign * k) for k in (1, 2, 3)]
    targets = [along_y(sign * k) for k in (1, -2, 3)]

    barrier = pltpu.get_barrier_semaphore()

    def greet(target):
        pl.semaphore_signal(barrier, inc=1, device_id=target, device_id_type=MESH)

    for k in range(1, peers):
        greet((d, lax.rem(j + k, peers)))
    for k in range(1, nx):
        greet((z * nx + lax.rem(x + k, nx), j))
    for k in range(1, nz):
        greet((lax.rem(z + k, nz) * nx + x, j))

    def placed(batch):
        chosen = slots_ref[batch]
        return jnp.where(chosen >= 0, routes_ref[batch] * cap + chosen, -1)

    for batch in range(batches):
        place = placed(batch)
        probs = probs_ref[batch].astype(F32)
        at = iota((slot_rows, toks), 0)
        picked = jnp.zeros((slot_rows, toks), F32)
        weight = jnp.zeros((slot_rows, toks), F32)
        for k in range(choose):
            same = at == place[k : k + 1, :]
            picked = jnp.where(same, 1.0, picked)
            weight = jnp.where(same, probs[k : k + 1, :], weight)
        sel[batch] = picked.astype(BF16)
        column = jnp.sum(weight, axis=1, keepdims=True)
        count = counts_ref[0, batch].astype(F32)
        block = jnp.where(iota((slot_rows, 128), 1) < 64, column, count)
        outw[:, batch] = block.astype(BF16).reshape(window, cap, 128)
    roww[:, y, c] = outw[mine]

    def remote(src, dst, send, recv, target):
        return pltpu.make_async_remote_copy(
            src_ref=src, dst_ref=dst, send_sem=send, recv_sem=recv, device_id=target, device_id_type=MESH
        )

    def send_own(source, target, step):
        for k in range(3):
            remote(
                source.at[lax.div(targets[k], 2)], target.at[:, y, c],
                near_s.at[step, k], near_r.at[step, k], (d, targets[k] * 2 + c),
            ).start()
        remote(source.at[mine], target.at[:, y, c], mate_s.at[step, 0], mate_r.at[step, 0], mate).start()

    def pass_near(target, step):
        for k in range(3):
            held = target.at[:, sources[k], c]
            remote(held, held, near_s.at[step, k], near_r.at[step, k], mate).wait_recv()
            remote(held, held, mate_s.at[step, k + 1], mate_r.at[step, k + 1], mate).start()

    def pass_mate(target, step):
        for k in range(4):
            held = target.at[:, along_y(-sign * (k + 1)), c]
            remote(held, held, mate_s.at[step, k], mate_r.at[step, k], mate).wait_recv()
        half = target.at[:, :, c]
        remote(half, half, sib_s.at[step], sib_r.at[step], sibling).start()

    def take_sibling(target, step):
        half = target.at[:, :, 1 - c]
        remote(half, half, sib_s.at[step], sib_r.at[step], sibling).wait_recv()

    def finish_sends(source, target, step):
        for k in range(3):
            remote(source.at[0], source.at[0], near_s.at[step, k], near_r.at[step, k], mate).wait_send()
        for k in range(4):
            remote(source.at[0], source.at[0], mate_s.at[step, k], mate_r.at[step, k], mate).wait_send()
        half = target.at[:, :, c]
        remote(half, half, sib_s.at[step], sib_r.at[step], sibling).wait_send()

    def owner(step):
        return lax.rem(z + 1 + step, nz)

    def columns(step):
        return pl.ds(pl.multiple_of(owner(step) * cw, cw), cw)

    def prepare(step):
        for batch in range(batches):
            block = jnp.dot(sel[batch], dout_ref[batch, :, columns(step)], preferred_element_type=F32)
            out[step, :, batch] = block.astype(BF16).reshape(window, cap, cw)
        rows[step, :, y, c] = out[step, mine]

    def compute(step):
        held = rows[step].reshape(total_rows, cw)
        back[...] += lax.dot_general(
            w_ref[:, columns(step)], held, (((1,), (1,)), ((), ())), preferred_element_type=F32
        )
        wide = jnp.concatenate([wmat[...]] * (cw // 128), axis=1) if cw > 128 else wmat[:, :cw]
        weighted = (wide * held.astype(F32)).astype(BF16)
        term = jnp.dot(ht[...], weighted, preferred_element_type=F32)
        flat = jnp.transpose(term)
        depth = cw // nx
        first = flat[:, :128].reshape(nx, depth, 128)
        last = flat[:, 128:].reshape(nx, 2, depth // 2, hidden - 128)
        packed = jnp.concatenate([last[:, 0], last[:, 1]], axis=-1)
        xs[step] = jnp.concatenate([first, packed], axis=1).astype(BF16)
        for k in range(1, nx):
            there = lax.rem(x + k, nx)
            remote(
                xs.at[step, there], xr.at[step, k - 1], x_s.at[step], x_r.at[step], (z * nx + there, j)
            ).start()

    def combine(step):
        remote(xr.at[step], xr.at[step], x_s.at[step], x_r.at[step], mate).wait_recv()
        summed = xs[step, x].astype(F32)
        for k in range(nx - 1):
            summed = summed + xr[step, k].astype(F32)
        zs[step] = summed

    def send_z(step):
        remote(zs.at[step], zr.at[step], z_s.at[step], z_r.at[step], (owner(step) * nx + x, j)).start()

    for step in range(AHEAD):
        prepare(step)
    for batch in range(batches):
        width = peers * cap
        ht[:, batch * width : (batch + 1) * width] = hid_ref[batch]
    back[...] = jnp.zeros_like(back)

    pl.semaphore_wait(barrier, peers - 1 + nx - 1 + nz - 1)
    send_own(outw, roww, nz)
    for step in range(AHEAD):
        send_own(out.at[step], rows.at[step], step)
    pass_near(roww, nz)
    pass_mate(roww, nz)

    def weights_arrive():
        take_sibling(roww, nz)
        flat = roww[...].reshape(total_rows, 128)
        wide = flat.astype(F32)
        wmat[...] = jnp.broadcast_to(wide[:, 0:1], wmat.shape)
        first = (iota((8, 128), 1) == 0).astype(BF16)
        wrow[...] = lax.dot_general(first, flat, (((1,), (1,)), ((), ())), preferred_element_type=F32)
        count = jnp.sum(wide[:, 64:65], axis=0, keepdims=True) * (1.0 / cap)
        cs[0] = jnp.broadcast_to(count, cs.shape[1:])
        for k in range(1, nx):
            remote(cs.at[0], cxr.at[k - 1], c_s.at[0], c_r.at[0], (z * nx + lax.rem(x + k, nx), j)).start()

    def counts_second():
        remote(cxr, cxr, c_s.at[0], c_r.at[0], mate).wait_recv()
        cs[1] = cs[0] + jnp.sum(cxr[...], axis=0)
        for k in range(1, nz):
            remote(cs.at[1], czr.at[k - 1], c_s.at[1], c_r.at[1], (lax.rem(z + k, nz) * nx + x, j)).start()

    def body(i, carry):
        @pl.when(i + AHEAD < nz)
        def _():
            prepare(i + AHEAD)
            send_own(out.at[i + AHEAD], rows.at[i + AHEAD], i + AHEAD)

        @pl.when(i < nz)
        def _():
            pass_near(rows.at[i], i)

        @pl.when((i >= 1) & (i < nz + 1))
        def _():
            pass_mate(rows.at[i - 1], i - 1)

        @pl.when(i == 1)
        def _():
            weights_arrive()

        @pl.when(i == min(4, nz))
        def _():
            counts_second()

        @pl.when((i >= 2) & (i < nz + 2))
        def _():
            take_sibling(rows.at[i - 2], i - 2)
            compute(i - 2)

        @pl.when((i >= 3) & (i < nz + 2))
        def _():
            combine(i - 3)
            send_z(i - 3)

        return carry

    lax.fori_loop(0, nz + 2, body, 0)

    grads = back[...]
    partial = jnp.sum(ht[...].astype(F32) * grads, axis=0, keepdims=True)
    lane = iota((peers, total_rows), 1)
    spread = jnp.where(lax.rem(lax.div(lane, cap), peers) == iota((peers, total_rows), 0), partial, 0.0)
    row = iota((total_rows, 128), 0)
    place = mine * (batches * cap) + lax.div(row, peers * cap) * cap + lax.rem(row, cap)
    gather = (iota((total_rows, 128), 1) == place).astype(F32)
    back_rows = jnp.dot(spread, gather, precision=lax.Precision.HIGHEST, preferred_element_type=F32)
    for k in range(peers):
        rs[k] = back_rows[k : k + 1, :]
    for k in range(1, peers):
        there = lax.rem(j + k, peers)
        remote(rs.at[there], rr.at[k - 1], ret_s, ret_r, (d, there)).start()

    remote(czr, czr, c_s.at[1], c_r.at[1], mate).wait_recv()
    token_total = jnp.sum((cs[1] + jnp.sum(czr[...], axis=0))[0:1, 0:1], axis=0, keepdims=True)
    grad_scale = scale_top / token_total

    scaled = ((grad_scale * wrow[0:1, :]) * grads).astype(BF16)
    for batch in range(batches):
        width = peers * cap
        dh_ref[batch] = scaled[:, batch * width : (batch + 1) * width]

    combine(nz - 1)
    for step in range(nz - 1):
        remote(zr.at[step], zr.at[step], z_s.at[step], z_r.at[step], mate).wait_recv()
    share = zs[nz - 1]
    for step in range(nz - 1):
        share = share + zr[step]
    share = grad_scale * share
    depth = dw_ref.shape[0]
    dw_ref[:, :128] = share[:depth]
    dw_ref[: depth // 2, 128:] = share[depth:, : hidden - 128]
    dw_ref[depth // 2 :, 128:] = share[depth:, hidden - 128 :]

    remote(rr, rr, ret_s, ret_r, mate).wait_recv()
    totals = rs[j]
    for k in range(peers - 1):
        totals = totals + rr[k]
    diagonal = iota((128, 128), 0) == iota((128, 128), 1)
    column = jnp.sum(jnp.where(diagonal, totals, 0.0), axis=1, keepdims=True)
    for batch in range(batches):
        place = placed(batch)
        mine_column = jnp.concatenate(
            [column[(e * batches + batch) * cap : (e * batches + batch + 1) * cap] for e in range(window)], axis=0
        )
        at = iota((slot_rows, toks), 0)
        for k in range(choose):
            found = jnp.sum(jnp.where(at == place[k : k + 1, :], mine_column, 0.0), axis=0, keepdims=True)
            dp_ref[batch, k : k + 1, :] = grad_scale * found

    finish_sends(outw, roww, nz)
    for step in range(nz):
        finish_sends(out.at[step], rows.at[step], step)
        remote(xr.at[step], xr.at[step], x_s.at[step], x_r.at[step], mate).wait_send()
    for step in range(nz - 1):
        remote(zs.at[step], zs.at[step], z_s.at[step], z_r.at[step], mate).wait_send()
    remote(cxr, cxr, c_s.at[0], c_r.at[0], mate).wait_send()
    remote(czr, czr, c_s.at[1], c_r.at[1], mate).wait_send()
    remote(rr, rr, ret_s, ret_r, mate).wait_send()


def on_device(nz, nx, d_out, routes, slots, route_probs, token_counts, hidden, w_down):
    batches, toks, choose = routes.shape
    features = d_out.shape[2]
    units, slot_count = hidden.shape[3], hidden.shape[2]
    peers = 2 * RING
    cap = slot_count // peers
    window = peers // GROUP
    cw = features // nz
    total_rows = batches * slot_count
    piece = (features // (nz * nx)) * units // 128
    scale_top = float(batches * toks * nz * nx * peers)
    dma = pltpu.SemaphoreType.DMA
    vmem = pl.BlockSpec(memory_space=pltpu.VMEM)
    dh, dw, dp = pl.pallas_call(
        functools.partial(kernel, nz, nx, scale_top),
        out_shape=(
            jax.ShapeDtypeStruct((batches, units, slot_count), BF16),
            jax.ShapeDtypeStruct((features // (nz * nx), units), F32),
            jax.ShapeDtypeStruct((batches, choose, toks), F32),
        ),
        in_specs=[vmem] * 4 + [pl.BlockSpec(memory_space=pltpu.SMEM)] + [vmem] * 2,
        out_specs=[vmem] * 3,
        scratch_shapes=[
            pltpu.VMEM((batches, window * cap, toks), BF16),
            pltpu.VMEM((nz, window, batches, cap, cw), BF16),
            pltpu.VMEM((window, batches, cap, 128), BF16),
            pltpu.VMEM((nz, batches, RING, 2, cap, cw), BF16),
            pltpu.VMEM((batches, RING, 2, cap, 128), BF16),
            pltpu.VMEM((total_rows, 128), F32),
            pltpu.VMEM((8, total_rows), F32),
            pltpu.VMEM((units, total_rows), F32),
            pltpu.VMEM((units, total_rows), BF16),
            pltpu.VMEM((nz, nx, piece, 128), BF16),
            pltpu.VMEM((nz, nx - 1, piece, 128), BF16),
            pltpu.VMEM((nz, piece, 128), F32),
            pltpu.VMEM((nz - 1, piece, 128), F32),
            pltpu.VMEM((2, 8, 128), F32),
            pltpu.VMEM((nx - 1, 8, 128), F32),
            pltpu.VMEM((nz - 1, 8, 128), F32),
            pltpu.VMEM((peers, 1, 128), F32),
            pltpu.VMEM((peers - 1, 1, 128), F32),
            dma((nz + 1, 3)), dma((nz + 1, 3)), dma((nz + 1, 4)), dma((nz + 1, 4)),
            dma((nz + 1,)), dma((nz + 1,)), dma((nz,)), dma((nz,)),
            dma((nz,)), dma((nz,)), dma((2,)), dma((2,)), dma, dma,
        ],
        compiler_params=pltpu.CompilerParams(
            collective_id=0, has_side_effects=True, vmem_limit_bytes=32 * 1024 * 1024
        ),
    )(
        d_out,
        jnp.swapaxes(routes, 1, 2),
        jnp.swapaxes(slots, 1, 2),
        jnp.swapaxes(route_probs, 1, 2),
        jnp.swapaxes(token_counts, 0, 1),
        jnp.swapaxes(hidden[:, 0], 1, 2),
        w_down,
    )
    return jnp.swapaxes(dh, 1, 2)[:, None], dw, jnp.swapaxes(dp, 1, 2)


def solution(mesh):
    nx = math.isqrt(mesh.shape["dp"])
    nz = mesh.shape["dp"] // nx
    both = ("dp", "expert")
    in_specs = (
        P(None, both, None),
        P(None, both, None),
        P(None, both, None),
        P(None, both, None),
        P(None, both),
        P(None, "dp", None, "expert"),
        P("expert", None),
    )
    out_specs = (P(None, "dp", None, "expert"), P("dp", "expert"), P(None, both, None))
    return jax.shard_map(
        functools.partial(on_device, nz, nx), mesh=mesh, in_specs=in_specs, out_specs=out_specs, check_vma=False
    )
```

```python
import functools
import math

import jax
import jax.numpy as jnp
from jax import lax
from jax.experimental import pallas as pl
from jax.experimental.pallas import tpu as pltpu
from jax.sharding import PartitionSpec as P

MESH = pl.DeviceIdType.MESH
F32 = jnp.float32
BF16 = jnp.bfloat16
RING = 8
GROUP = 4
AHEAD = 8
MATE_LAG = 2
SIB_LAG = 1
SUM_LAG = 6


def iota(shape, dimension):
    return lax.broadcasted_iota(jnp.int32, shape, dimension)


def kernel(
    nz, nx, scale_top,
    dout_hbm, routes_hbm, slots_hbm, probs_hbm, counts_ref, hid_hbm, w_hbm,
    dh_ref, dw_ref, dp_ref,
    dout_ref, routes_ref, slots_ref, probs_ref, ht, w_ref, in_sem,
    sel, out, outw, rows, roww, wmat, wrow, back, spot, xs, xr, zs, zr, zb, zbr, zx, zxr, cs, cxr, czr, rs, rr,
    near_s, near_r, mate_s, mate_r, sib_s, sib_r, x_s, x_r, z_s, z_r, b_s, b_r, f_s, f_r, c_s, c_r, ret_s, ret_r,
):
    d = lax.axis_index("dp")
    j = lax.axis_index("expert")
    z, x = lax.div(d, nx), lax.rem(d, nx)
    y, c = lax.div(j, 2), lax.rem(j, 2)
    sign = 2 * lax.rem(y, 2) - 1
    mine = lax.div(y, 2)
    batches, choose, toks = routes_ref.shape
    hidden = w_ref.shape[0]
    cap = out.shape[3]
    cw = out.shape[4]
    peers = 2 * RING
    window = peers // GROUP
    slot_rows = window * cap
    total_rows = batches * peers * cap

    def along_y(offset):
        return lax.rem(y + offset + 2 * RING, RING)

    mate_y = y - sign
    mate = (d, mate_y * 2 + c)
    sibling = (d, y * 2 + 1 - c)
    sources = [along_y(sign * k) for k in (1, 2, 3)]
    targets = [along_y(sign * k) for k in (1, -2, 3)]

    width = peers * cap
    loads = [
        pltpu.make_async_copy(src, dst, in_sem.at[k])
        for k, (src, dst) in enumerate(
            [(routes_hbm, routes_ref), (slots_hbm, slots_ref), (probs_hbm, probs_ref), (dout_hbm, dout_ref)]
            + [(hid_hbm.at[batch], ht.at[:, batch * width : (batch + 1) * width]) for batch in range(batches)]
            + [(w_hbm, w_ref)]
        )
    ]
    for load in loads:
        load.start()

    barrier = pltpu.get_barrier_semaphore()

    def greet(target):
        pl.semaphore_signal(barrier, inc=1, device_id=target, device_id_type=MESH)

    for k in range(1, peers):
        greet((d, lax.rem(j + k, peers)))
    for k in range(1, nx):
        greet((z * nx + lax.rem(x + k, nx), j))
    for k in range(1, nz):
        greet((lax.rem(z + k, nz) * nx + x, j))

    def placed(batch):
        chosen = slots_ref[batch]
        return jnp.where(chosen >= 0, routes_ref[batch] * cap + chosen, -1)

    for load in loads[:3]:
        load.wait()
    weights = []
    for batch in range(batches):
        place = placed(batch)
        probs = probs_ref[batch].astype(F32)
        at = iota((slot_rows, toks), 0)
        picked = jnp.zeros((slot_rows, toks), F32)
        weight = jnp.zeros((slot_rows, toks), F32)
        for k in range(choose):
            same = at == place[k : k + 1, :]
            picked = jnp.where(same, 1.0, picked)
            weight = jnp.where(same, probs[k : k + 1, :], weight)
        sel[batch] = picked.astype(BF16)
        weights.append(weight)

    def send_weights():
        for batch in range(batches):
            column = jnp.sum(weights[batch], axis=1, keepdims=True)
            count = counts_ref[0, batch].astype(F32)
            block = jnp.where(iota((slot_rows, 128), 1) < 64, column, count)
            outw[:, batch] = block.astype(BF16).reshape(window, cap, 128)
        roww[:, y, c] = outw[mine]
        send_own(outw, roww, nz)

    def remote(src, dst, send, recv, target):
        return pltpu.make_async_remote_copy(
            src_ref=src, dst_ref=dst, send_sem=send, recv_sem=recv, device_id=target, device_id_type=MESH
        )

    def send_own(source, target, step):
        for k in range(3):
            remote(
                source.at[lax.div(targets[k], 2)], target.at[:, y, c],
                near_s.at[step, k], near_r.at[step, k], (d, targets[k] * 2 + c),
            ).start()
        remote(source.at[mine], target.at[:, y, c], mate_s.at[step, 0], mate_r.at[step, 0], mate).start()

    def pass_near(target, step):
        for k in range(3):
            held = target.at[:, sources[k], c]
            remote(held, held, near_s.at[step, k], near_r.at[step, k], mate).wait_recv()
            remote(held, held, mate_s.at[step, k + 1], mate_r.at[step, k + 1], mate).start()

    def pass_mate(target, step):
        for k in range(4):
            held = target.at[:, along_y(-sign * (k + 1)), c]
            remote(held, held, mate_s.at[step, k], mate_r.at[step, k], mate).wait_recv()
        half = target.at[:, :, c]
        remote(half, half, sib_s.at[step], sib_r.at[step], sibling).start()

    def take_sibling(target, step):
        half = target.at[:, :, 1 - c]
        remote(half, half, sib_s.at[step], sib_r.at[step], sibling).wait_recv()

    def finish_sends(source, target, step):
        for k in range(3):
            remote(source.at[0], source.at[0], near_s.at[step, k], near_r.at[step, k], mate).wait_send()
        for k in range(4):
            remote(source.at[0], source.at[0], mate_s.at[step, k], mate_r.at[step, k], mate).wait_send()
        half = target.at[:, :, c]
        remote(half, half, sib_s.at[step], sib_r.at[step], sibling).wait_send()

    def owner(step):
        return lax.rem(z + 1 + step, nz)

    def columns(step):
        return pl.ds(pl.multiple_of(owner(step) * cw, cw), cw)

    def prepare(step):
        for batch in range(batches):
            block = jnp.dot(sel[batch], dout_ref[batch, :, columns(step)], preferred_element_type=F32)
            out[step, :, batch] = block.astype(BF16).reshape(window, cap, cw)
        rows[step, :, y, c] = out[step, mine]

    def compute(step):
        held = rows[step].reshape(total_rows, cw)
        back[...] += lax.dot_general(
            w_ref[:, columns(step)], held, (((1,), (1,)), ((), ())), preferred_element_type=F32
        )
        wide = jnp.concatenate([wmat[...]] * (cw // 128), axis=1) if cw > 128 else wmat[:, :cw]
        weighted = (wide * held.astype(F32)).astype(BF16)
        term = jnp.dot(ht[...], weighted, preferred_element_type=F32)
        flat = jnp.transpose(term)
        depth = cw // nx
        first = flat[:, :128].reshape(nx, depth, 128)
        last = flat[:, 128:].reshape(nx, 2, depth // 2, hidden - 128)
        packed = jnp.concatenate([last[:, 0], last[:, 1]], axis=-1)
        xs[step] = first.astype(BF16)
        zb[step] = packed.astype(BF16)
        for k in range(1, nx):
            there = lax.rem(x + k, nx)
            remote(
                xs.at[step, there], xr.at[step, k - 1], x_s.at[step], x_r.at[step], (z * nx + there, j)
            ).start()

        @pl.when(step < nz - 1)
        def _():
            remote(zb.at[step], zbr.at[step], b_s.at[step], b_r.at[step], (owner(step) * nx + x, j)).start()

    def combine(step):
        remote(xr.at[step], xr.at[step], x_s.at[step], x_r.at[step], mate).wait_recv()
        summed = xs[step, x].astype(F32)
        for k in range(nx - 1):
            summed = summed + xr[step, k].astype(F32)
        zs[step] = summed

    def send_z(step):
        remote(zs.at[step], zr.at[step], z_s.at[step], z_r.at[step], (owner(step) * nx + x, j)).start()

    loads[3].wait()
    prepare(0)
    pl.semaphore_wait(barrier, peers - 1 + nx - 1 + nz - 1)
    send_own(out.at[0], rows.at[0], 0)
    send_weights()
    for step in range(1, min(AHEAD, nz)):
        prepare(step)
        send_own(out.at[step], rows.at[step], step)
    back[...] = jnp.zeros_like(back)
    row = iota((total_rows, 128), 0)
    shift, mask = cap.bit_length() - 1, cap - 1
    place = mine * (batches * cap) + (row >> (2 * shift)) * cap + (row & mask)
    spot[...] = (iota((total_rows, 128), 1) == place).astype(F32)
    for load in loads[4:]:
        load.wait()

    def weights_arrive():
        take_sibling(roww, nz)
        flat = roww[...].reshape(total_rows, 128)
        wide = flat.astype(F32)
        wmat[...] = jnp.broadcast_to(wide[:, 0:1], wmat.shape)
        first = (iota((8, 128), 1) == 0).astype(BF16)
        wrow[...] = lax.dot_general(first, flat, (((1,), (1,)), ((), ())), preferred_element_type=F32)
        count = jnp.sum(wide[:, 64:65], axis=0, keepdims=True) * (1.0 / cap)
        cs[0] = jnp.broadcast_to(count, cs.shape[1:])
        for k in range(1, nx):
            remote(cs.at[0], cxr.at[k - 1], c_s.at[0], c_r.at[0], (z * nx + lax.rem(x + k, nx), j)).start()

    def counts_second():
        remote(cxr, cxr, c_s.at[0], c_r.at[0], mate).wait_recv()
        cs[1] = cs[0] + jnp.sum(cxr[...], axis=0)
        for k in range(1, nz):
            remote(cs.at[1], czr.at[k - 1], c_s.at[1], c_r.at[1], (lax.rem(z + k, nz) * nx + x, j)).start()

    def body(i, carry):
        if AHEAD < nz:

            @pl.when(i + AHEAD < nz)
            def _():
                prepare(i + AHEAD)
                send_own(out.at[i + AHEAD], rows.at[i + AHEAD], i + AHEAD)

        @pl.when(i < nz)
        def _():
            pass_near(rows.at[i], i)

        @pl.when(i == 0)
        def _():
            pass_near(roww, nz)

        held = i - MATE_LAG

        @pl.when((held >= 0) & (held < nz))
        def _():
            pass_mate(rows.at[held], held)

        @pl.when(held == 0)
        def _():
            pass_mate(roww, nz)

        whole = held - SIB_LAG

        @pl.when(whole == 0)
        def _():
            weights_arrive()

        @pl.when(i == nz)
        def _():
            counts_second()

        @pl.when((whole >= 0) & (whole < nz))
        def _():
            take_sibling(rows.at[whole], whole)
            compute(whole)

        done = whole - SUM_LAG

        @pl.when((done >= 0) & (done < nz - 1))
        def _():
            combine(done)
            send_z(done)

        return carry

    lax.fori_loop(0, nz + max(MATE_LAG + SIB_LAG, MATE_LAG + SIB_LAG + SUM_LAG - 1), body, 0)

    for step in range(nz - 1):
        remote(zbr.at[step], zbr.at[step], b_s.at[step], b_r.at[step], mate).wait_recv()
    block = zb[nz - 1].astype(F32)
    for step in range(nz - 1):
        block = block + zbr[step].astype(F32)
    zx[...] = block
    for k in range(1, nx):
        there = lax.rem(x + k, nx)
        remote(zx.at[there], zxr.at[k - 1], f_s, f_r, (z * nx + there, j)).start()

    grads = back[...]
    partial = jnp.sum(ht[...].astype(F32) * grads, axis=0, keepdims=True)
    lane = iota((peers, total_rows), 1)
    spread = jnp.where(((lane >> shift) & (peers - 1)) == iota((peers, total_rows), 0), partial, 0.0)
    back_rows = jnp.dot(spread, spot[...], precision=lax.Precision.HIGHEST, preferred_element_type=F32)
    for k in range(peers):
        rs[k] = back_rows[k : k + 1, :]
    for k in range(1, peers):
        there = lax.rem(j + k, peers)
        remote(rs.at[there], rr.at[k - 1], ret_s, ret_r, (d, there)).start()

    remote(czr, czr, c_s.at[1], c_r.at[1], mate).wait_recv()
    token_total = jnp.sum((cs[1] + jnp.sum(czr[...], axis=0))[0:1, 0:1], axis=0, keepdims=True)
    grad_scale = scale_top / token_total

    scaled = ((grad_scale * wrow[0:1, :]) * grads).astype(BF16)
    for batch in range(batches):
        dh_ref[batch] = scaled[:, batch * width : (batch + 1) * width]

    combine(nz - 1)
    for step in range(nz - 1):
        remote(zr.at[step], zr.at[step], z_s.at[step], z_r.at[step], mate).wait_recv()
    share = zs[nz - 1]
    for step in range(nz - 1):
        share = share + zr[step]
    dw_ref[:, :128] = grad_scale * share
    remote(zxr, zxr, f_s, f_r, mate).wait_recv()
    share = zx[x]
    for k in range(nx - 1):
        share = share + zxr[k]
    share = grad_scale * share
    depth = dw_ref.shape[0]
    dw_ref[: depth // 2, 128:] = share[:, : hidden - 128]
    dw_ref[depth // 2 :, 128:] = share[:, hidden - 128 :]

    remote(rr, rr, ret_s, ret_r, mate).wait_recv()
    totals = rs[j]
    for k in range(peers - 1):
        totals = totals + rr[k]
    diagonal = iota((128, 128), 0) == iota((128, 128), 1)
    column = jnp.sum(jnp.where(diagonal, totals, 0.0), axis=1, keepdims=True)
    for batch in range(batches):
        place = placed(batch)
        mine_column = jnp.concatenate(
            [column[(e * batches + batch) * cap : (e * batches + batch + 1) * cap] for e in range(window)], axis=0
        )
        at = iota((slot_rows, toks), 0)
        for k in range(choose):
            found = jnp.sum(jnp.where(at == place[k : k + 1, :], mine_column, 0.0), axis=0, keepdims=True)
            dp_ref[batch, k : k + 1, :] = grad_scale * found

    finish_sends(outw, roww, nz)
    for step in range(nz):
        finish_sends(out.at[step], rows.at[step], step)
        remote(xr.at[step], xr.at[step], x_s.at[step], x_r.at[step], mate).wait_send()
    for step in range(nz - 1):
        remote(zs.at[step], zs.at[step], z_s.at[step], z_r.at[step], mate).wait_send()
        remote(zb.at[step], zb.at[step], b_s.at[step], b_r.at[step], mate).wait_send()
    remote(zxr, zxr, f_s, f_r, mate).wait_send()
    remote(cxr, cxr, c_s.at[0], c_r.at[0], mate).wait_send()
    remote(czr, czr, c_s.at[1], c_r.at[1], mate).wait_send()
    remote(rr, rr, ret_s, ret_r, mate).wait_send()


def on_device(nz, nx, d_out, routes, slots, route_probs, token_counts, hidden, w_down):
    batches, toks, choose = routes.shape
    features = d_out.shape[2]
    units, slot_count = hidden.shape[3], hidden.shape[2]
    peers = 2 * RING
    cap = slot_count // peers
    window = peers // GROUP
    cw = features // nz
    total_rows = batches * slot_count
    depth = features // (nz * nx)
    half = depth * (units - 128) // 128
    scale_top = float(batches * toks * nz * nx * peers)
    dma = pltpu.SemaphoreType.DMA
    vmem = pl.BlockSpec(memory_space=pltpu.VMEM)
    hbm = pl.BlockSpec(memory_space=pltpu.HBM)
    dh, dw, dp = pl.pallas_call(
        functools.partial(kernel, nz, nx, scale_top),
        out_shape=(
            jax.ShapeDtypeStruct((batches, units, slot_count), BF16),
            jax.ShapeDtypeStruct((features // (nz * nx), units), F32),
            jax.ShapeDtypeStruct((batches, choose, toks), F32),
        ),
        in_specs=[hbm] * 4 + [pl.BlockSpec(memory_space=pltpu.SMEM)] + [hbm] * 2,
        out_specs=[vmem] * 3,
        scratch_shapes=[
            pltpu.VMEM((batches, toks, features), BF16),
            pltpu.VMEM((batches, choose, toks), jnp.int32),
            pltpu.VMEM((batches, choose, toks), jnp.int32),
            pltpu.VMEM((batches, choose, toks), BF16),
            pltpu.VMEM((units, total_rows), BF16),
            pltpu.VMEM((units, features), BF16),
            dma((5 + batches,)),
            pltpu.VMEM((batches, window * cap, toks), BF16),
            pltpu.VMEM((nz, window, batches, cap, cw), BF16),
            pltpu.VMEM((window, batches, cap, 128), BF16),
            pltpu.VMEM((nz, batches, RING, 2, cap, cw), BF16),
            pltpu.VMEM((batches, RING, 2, cap, 128), BF16),
            pltpu.VMEM((total_rows, 128), F32),
            pltpu.VMEM((8, total_rows), F32),
            pltpu.VMEM((units, total_rows), F32),
            pltpu.VMEM((total_rows, 128), F32),
            pltpu.VMEM((nz, nx, depth, 128), BF16),
            pltpu.VMEM((nz, nx - 1, depth, 128), BF16),
            pltpu.VMEM((nz, depth, 128), F32),
            pltpu.VMEM((nz - 1, depth, 128), F32),
            pltpu.VMEM((nz, nx, half, 128), BF16),
            pltpu.VMEM((nz - 1, nx, half, 128), BF16),
            pltpu.VMEM((nx, half, 128), F32),
            pltpu.VMEM((nx - 1, half, 128), F32),
            pltpu.VMEM((2, 8, 128), F32),
            pltpu.VMEM((nx - 1, 8, 128), F32),
            pltpu.VMEM((nz - 1, 8, 128), F32),
            pltpu.VMEM((peers, 1, 128), F32),
            pltpu.VMEM((peers - 1, 1, 128), F32),
            dma((nz + 1, 3)), dma((nz + 1, 3)), dma((nz + 1, 4)), dma((nz + 1, 4)),
            dma((nz + 1,)), dma((nz + 1,)), dma((nz,)), dma((nz,)),
            dma((nz,)), dma((nz,)), dma((nz,)), dma((nz,)), dma, dma, dma((2,)), dma((2,)), dma, dma,
        ],
        compiler_params=pltpu.CompilerParams(
            collective_id=0, has_side_effects=True, vmem_limit_bytes=60 * 1024 * 1024
        ),
    )(
        d_out,
        jnp.swapaxes(routes, 1, 2),
        jnp.swapaxes(slots, 1, 2),
        jnp.swapaxes(route_probs, 1, 2),
        jnp.swapaxes(token_counts, 0, 1),
        jnp.swapaxes(hidden[:, 0], 1, 2),
        w_down,
    )
    return jnp.swapaxes(dh, 1, 2)[:, None], dw, jnp.swapaxes(dp, 1, 2)


def solution(mesh):
    nx = math.isqrt(mesh.shape["dp"])
    nz = mesh.shape["dp"] // nx
    both = ("dp", "expert")
    in_specs = (
        P(None, both, None),
        P(None, both, None),
        P(None, both, None),
        P(None, both, None),
        P(None, both),
        P(None, "dp", None, "expert"),
        P("expert", None),
    )
    out_specs = (P(None, "dp", None, "expert"), P("dp", "expert"), P(None, both, None))
    return jax.shard_map(
        functools.partial(on_device, nz, nx), mesh=mesh, in_specs=in_specs, out_specs=out_specs, check_vma=False
    )
```

```python
import functools
import math

import jax
import jax.numpy as jnp
from jax import lax
from jax.experimental import pallas as pl
from jax.experimental.pallas import tpu as pltpu
from jax.sharding import PartitionSpec as P

MESH = pl.DeviceIdType.MESH
F32 = jnp.float32
BF16 = jnp.bfloat16
RING = 8
GROUP = 4
AHEAD = 8
MATE_LAG = 2
SIB_LAG = 1
SUM_LAG = 6


def iota(shape, dimension):
    return lax.broadcasted_iota(jnp.int32, shape, dimension)


def kernel(
    nz, nx, scale_top,
    dout_hbm, routes_hbm, slots_hbm, probs_hbm, counts_ref, hid_hbm, w_hbm,
    dh_ref, dw_ref, dp_ref,
    dout_ref, routes_ref, slots_ref, probs_ref, ht, w_ref, in_sem,
    sel, out, outw, rows, roww, wmat, wrow, back, spot, xs, xr, zs, zr, zb, zbr, zx, zxr, cs, cxr, czr, rs, rr,
    near_s, near_r, mate_s, mate_r, sib_s, sib_r, x_s, x_r, z_s, z_r, b_s, b_r, f_s, f_r, c_s, c_r, ret_s, ret_r,
):
    d = lax.axis_index("dp")
    j = lax.axis_index("expert")
    z, x = lax.div(d, nx), lax.rem(d, nx)
    y, c = lax.div(j, 2), lax.rem(j, 2)
    sign = 2 * lax.rem(y, 2) - 1
    mine = lax.div(y, 2)
    batches, choose, toks = routes_ref.shape
    hidden = w_ref.shape[0]
    cap = out.shape[3]
    cw = out.shape[4]
    peers = 2 * RING
    window = peers // GROUP
    slot_rows = window * cap
    total_rows = batches * peers * cap

    def along_y(offset):
        return lax.rem(y + offset + 2 * RING, RING)

    mate_y = y - sign
    mate = (d, mate_y * 2 + c)
    sibling = (d, y * 2 + 1 - c)
    sources = [along_y(sign * k) for k in (1, 2, 3)]
    targets = [along_y(sign * k) for k in (1, -2, 3)]

    width = peers * cap
    loads = [
        pltpu.make_async_copy(src, dst, in_sem.at[k])
        for k, (src, dst) in enumerate(
            [(routes_hbm, routes_ref), (slots_hbm, slots_ref), (probs_hbm, probs_ref), (dout_hbm, dout_ref)]
            + [(hid_hbm.at[batch], ht.at[:, batch * width : (batch + 1) * width]) for batch in range(batches)]
            + [(w_hbm, w_ref)]
        )
    ]
    for load in loads:
        load.start()

    barrier = pltpu.get_barrier_semaphore()

    def greet(target):
        pl.semaphore_signal(barrier, inc=1, device_id=target, device_id_type=MESH)

    for k in range(1, peers):
        greet((d, lax.rem(j + k, peers)))
    for k in range(1, nx):
        greet((z * nx + lax.rem(x + k, nx), j))
    for k in range(1, nz):
        greet((lax.rem(z + k, nz) * nx + x, j))

    def placed(batch):
        chosen = slots_ref[batch]
        return jnp.where(chosen >= 0, routes_ref[batch] * cap + chosen, -1)

    for load in loads[:3]:
        load.wait()
    weights = []
    for batch in range(batches):
        place = placed(batch)
        probs = probs_ref[batch].astype(F32)
        at = iota((slot_rows, toks), 0)
        picked = jnp.zeros((slot_rows, toks), F32)
        weight = jnp.zeros((slot_rows, toks), F32)
        for k in range(choose):
            same = at == place[k : k + 1, :]
            picked = jnp.where(same, 1.0, picked)
            weight = jnp.where(same, probs[k : k + 1, :], weight)
        sel[batch] = picked.astype(BF16)
        weights.append(weight)

    def send_weights():
        for batch in range(batches):
            column = jnp.sum(weights[batch], axis=1, keepdims=True)
            count = counts_ref[0, batch].astype(F32)
            block = jnp.where(iota((slot_rows, 128), 1) < 64, column, count)
            outw[:, batch] = block.astype(BF16).reshape(window, cap, 128)
        roww[:, y, c] = outw[mine]
        send_own(outw, roww, nz)

    def remote(src, dst, send, recv, target):
        return pltpu.make_async_remote_copy(
            src_ref=src, dst_ref=dst, send_sem=send, recv_sem=recv, device_id=target, device_id_type=MESH
        )

    def send_own(source, target, step):
        for k in range(3):
            remote(
                source.at[lax.div(targets[k], 2)], target.at[:, y, c],
                near_s.at[step, k], near_r.at[step, k], (d, targets[k] * 2 + c),
            ).start()
        remote(source.at[mine], target.at[:, y, c], mate_s.at[step, 0], mate_r.at[step, 0], mate).start()

    def pass_near(target, step):
        for k in range(3):
            held = target.at[:, sources[k], c]
            remote(held, held, near_s.at[step, k], near_r.at[step, k], mate).wait_recv()
            remote(held, held, mate_s.at[step, k + 1], mate_r.at[step, k + 1], mate).start()

    def pass_mate(target, step):
        for k in range(4):
            held = target.at[:, along_y(-sign * (k + 1)), c]
            remote(held, held, mate_s.at[step, k], mate_r.at[step, k], mate).wait_recv()
        half = target.at[:, :, c]
        remote(half, half, sib_s.at[step], sib_r.at[step], sibling).start()

    def take_sibling(target, step):
        half = target.at[:, :, 1 - c]
        remote(half, half, sib_s.at[step], sib_r.at[step], sibling).wait_recv()

    def finish_sends(source, target, step):
        for k in range(3):
            remote(source.at[0], source.at[0], near_s.at[step, k], near_r.at[step, k], mate).wait_send()
        for k in range(4):
            remote(source.at[0], source.at[0], mate_s.at[step, k], mate_r.at[step, k], mate).wait_send()
        half = target.at[:, :, c]
        remote(half, half, sib_s.at[step], sib_r.at[step], sibling).wait_send()

    def owner(step):
        return lax.rem(z + 1 + step, nz)

    def columns(step):
        return pl.ds(pl.multiple_of(owner(step) * cw, cw), cw)

    def prepare(step):
        for batch in range(batches):
            block = jnp.dot(sel[batch], dout_ref[batch, :, columns(step)], preferred_element_type=F32)
            out[step, :, batch] = block.astype(BF16).reshape(window, cap, cw)
        rows[step, :, y, c] = out[step, mine]

    def compute(step):
        held = rows[step].reshape(total_rows, cw)
        back[...] += lax.dot_general(
            w_ref[:, columns(step)], held, (((1,), (1,)), ((), ())), preferred_element_type=F32
        )
        wide = jnp.concatenate([wmat[...]] * (cw // 128), axis=1) if cw > 128 else wmat[:, :cw]
        weighted = (wide * held.astype(F32)).astype(BF16)
        term = jnp.dot(ht[...], weighted, preferred_element_type=F32)
        flat = jnp.transpose(term)
        depth = cw // nx
        first = flat[:, :128].reshape(nx, depth, 128)
        last = flat[:, 128:].reshape(nx, 2, depth // 2, hidden - 128)
        packed = jnp.concatenate([last[:, 0], last[:, 1]], axis=-1)
        xs[step] = first.astype(BF16)
        zb[step] = packed.astype(BF16)
        for k in range(1, nx):
            there = lax.rem(x + k, nx)
            remote(
                xs.at[step, there], xr.at[step, k - 1], x_s.at[step], x_r.at[step], (z * nx + there, j)
            ).start()

        @pl.when(step < nz - 1)
        def _():
            remote(zb.at[step], zbr.at[step], b_s.at[step], b_r.at[step], (owner(step) * nx + x, j)).start()

    def combine(step):
        remote(xr.at[step], xr.at[step], x_s.at[step], x_r.at[step], mate).wait_recv()
        summed = xs[step, x].astype(F32)
        for k in range(nx - 1):
            summed = summed + xr[step, k].astype(F32)
        zs[step] = summed

    def send_z(step):
        remote(zs.at[step], zr.at[step], z_s.at[step], z_r.at[step], (owner(step) * nx + x, j)).start()

    loads[3].wait()
    prepare(0)
    pl.semaphore_wait(barrier, peers - 1 + nx - 1 + nz - 1)
    send_own(out.at[0], rows.at[0], 0)
    send_weights()
    for step in range(1, min(AHEAD, nz)):
        prepare(step)
        send_own(out.at[step], rows.at[step], step)
    back[...] = jnp.zeros_like(back)
    row = iota((total_rows, 128), 0)
    shift, mask = cap.bit_length() - 1, cap - 1
    place = mine * (batches * cap) + (row >> (2 * shift)) * cap + (row & mask)
    spot[...] = (iota((total_rows, 128), 1) == place).astype(F32)
    for load in loads[4:]:
        load.wait()

    def weights_arrive():
        take_sibling(roww, nz)
        flat = roww[...].reshape(total_rows, 128)
        wide = flat.astype(F32)
        wmat[...] = jnp.broadcast_to(wide[:, 0:1], wmat.shape)
        first = (iota((8, 128), 1) == 0).astype(BF16)
        wrow[...] = lax.dot_general(first, flat, (((1,), (1,)), ((), ())), preferred_element_type=F32)
        count = jnp.sum(wide[:, 64:65], axis=0, keepdims=True) * (1.0 / cap)
        cs[0] = jnp.broadcast_to(count, cs.shape[1:])
        for k in range(1, nx):
            remote(cs.at[0], cxr.at[k - 1], c_s.at[0], c_r.at[0], (z * nx + lax.rem(x + k, nx), j)).start()

    def counts_second():
        remote(cxr, cxr, c_s.at[0], c_r.at[0], mate).wait_recv()
        cs[1] = cs[0] + jnp.sum(cxr[...], axis=0)
        for k in range(1, nz):
            remote(cs.at[1], czr.at[k - 1], c_s.at[1], c_r.at[1], (lax.rem(z + k, nz) * nx + x, j)).start()

    def body(i, carry):
        if AHEAD < nz:

            @pl.when(i + AHEAD < nz)
            def _():
                prepare(i + AHEAD)
                send_own(out.at[i + AHEAD], rows.at[i + AHEAD], i + AHEAD)

        @pl.when(i < nz)
        def _():
            pass_near(rows.at[i], i)

        @pl.when(i == 0)
        def _():
            pass_near(roww, nz)

        held = i - MATE_LAG

        @pl.when((held >= 0) & (held < nz))
        def _():
            pass_mate(rows.at[held], held)

        @pl.when(held == 0)
        def _():
            pass_mate(roww, nz)

        whole = held - SIB_LAG

        @pl.when(whole == 0)
        def _():
            weights_arrive()

        @pl.when(i == nz)
        def _():
            counts_second()

        @pl.when((whole >= 0) & (whole < nz))
        def _():
            take_sibling(rows.at[whole], whole)
            compute(whole)

        done = whole - SUM_LAG

        @pl.when((done >= 0) & (done < nz - 1))
        def _():
            combine(done)
            send_z(done)

        return carry

    lax.fori_loop(0, nz + MATE_LAG + SIB_LAG, body, 0)

    grads = back[...]
    partial = jnp.sum(ht[...].astype(F32) * grads, axis=0, keepdims=True)
    lane = iota((peers, total_rows), 1)
    spread = jnp.where(((lane >> shift) & (peers - 1)) == iota((peers, total_rows), 0), partial, 0.0)
    back_rows = jnp.dot(spread, spot[...], precision=lax.Precision.HIGHEST, preferred_element_type=F32)
    for k in range(peers):
        rs[k] = back_rows[k : k + 1, :]
    for k in range(1, peers):
        there = lax.rem(j + k, peers)
        remote(rs.at[there], rr.at[k - 1], ret_s, ret_r, (d, there)).start()

    for step in range(nz - 1):
        remote(zbr.at[step], zbr.at[step], b_s.at[step], b_r.at[step], mate).wait_recv()
    block = zb[nz - 1].astype(F32)
    for step in range(nz - 1):
        block = block + zbr[step].astype(F32)
    zx[...] = block
    for k in range(1, nx):
        there = lax.rem(x + k, nx)
        remote(zx.at[there], zxr.at[k - 1], f_s, f_r, (z * nx + there, j)).start()

    def rest(step, carry):
        combine(step)
        send_z(step)
        return carry

    lax.fori_loop(max(nz - SUM_LAG, 0), nz - 1, rest, 0)

    remote(czr, czr, c_s.at[1], c_r.at[1], mate).wait_recv()
    token_total = jnp.sum((cs[1] + jnp.sum(czr[...], axis=0))[0:1, 0:1], axis=0, keepdims=True)
    grad_scale = scale_top / token_total

    scaled = ((grad_scale * wrow[0:1, :]) * grads).astype(BF16)
    for batch in range(batches):
        dh_ref[batch] = scaled[:, batch * width : (batch + 1) * width]

    combine(nz - 1)
    for step in range(nz - 1):
        remote(zr.at[step], zr.at[step], z_s.at[step], z_r.at[step], mate).wait_recv()
    share = zs[nz - 1]
    for step in range(nz - 1):
        share = share + zr[step]
    dw_ref[:, :128] = grad_scale * share
    remote(zxr, zxr, f_s, f_r, mate).wait_recv()
    share = zx[x]
    for k in range(nx - 1):
        share = share + zxr[k]
    share = grad_scale * share
    depth = dw_ref.shape[0]
    dw_ref[: depth // 2, 128:] = share[:, : hidden - 128]
    dw_ref[depth // 2 :, 128:] = share[:, hidden - 128 :]

    remote(rr, rr, ret_s, ret_r, mate).wait_recv()
    totals = rs[j]
    for k in range(peers - 1):
        totals = totals + rr[k]
    diagonal = iota((128, 128), 0) == iota((128, 128), 1)
    column = jnp.sum(jnp.where(diagonal, totals, 0.0), axis=1, keepdims=True)
    for batch in range(batches):
        place = placed(batch)
        mine_column = jnp.concatenate(
            [column[(e * batches + batch) * cap : (e * batches + batch + 1) * cap] for e in range(window)], axis=0
        )
        at = iota((slot_rows, toks), 0)
        for k in range(choose):
            found = jnp.sum(jnp.where(at == place[k : k + 1, :], mine_column, 0.0), axis=0, keepdims=True)
            dp_ref[batch, k : k + 1, :] = grad_scale * found

    finish_sends(outw, roww, nz)
    for step in range(nz):
        finish_sends(out.at[step], rows.at[step], step)
        remote(xr.at[step], xr.at[step], x_s.at[step], x_r.at[step], mate).wait_send()
    for step in range(nz - 1):
        remote(zs.at[step], zs.at[step], z_s.at[step], z_r.at[step], mate).wait_send()
        remote(zb.at[step], zb.at[step], b_s.at[step], b_r.at[step], mate).wait_send()
    remote(zxr, zxr, f_s, f_r, mate).wait_send()
    remote(cxr, cxr, c_s.at[0], c_r.at[0], mate).wait_send()
    remote(czr, czr, c_s.at[1], c_r.at[1], mate).wait_send()
    remote(rr, rr, ret_s, ret_r, mate).wait_send()


def on_device(nz, nx, d_out, routes, slots, route_probs, token_counts, hidden, w_down):
    batches, toks, choose = routes.shape
    features = d_out.shape[2]
    units, slot_count = hidden.shape[3], hidden.shape[2]
    peers = 2 * RING
    cap = slot_count // peers
    window = peers // GROUP
    cw = features // nz
    total_rows = batches * slot_count
    depth = features // (nz * nx)
    half = depth * (units - 128) // 128
    scale_top = float(batches * toks * nz * nx * peers)
    dma = pltpu.SemaphoreType.DMA
    vmem = pl.BlockSpec(memory_space=pltpu.VMEM)
    hbm = pl.BlockSpec(memory_space=pltpu.HBM)
    dh, dw, dp = pl.pallas_call(
        functools.partial(kernel, nz, nx, scale_top),
        out_shape=(
            jax.ShapeDtypeStruct((batches, units, slot_count), BF16),
            jax.ShapeDtypeStruct((features // (nz * nx), units), F32),
            jax.ShapeDtypeStruct((batches, choose, toks), F32),
        ),
        in_specs=[hbm] * 4 + [pl.BlockSpec(memory_space=pltpu.SMEM)] + [hbm] * 2,
        out_specs=[vmem] * 3,
        scratch_shapes=[
            pltpu.VMEM((batches, toks, features), BF16),
            pltpu.VMEM((batches, choose, toks), jnp.int32),
            pltpu.VMEM((batches, choose, toks), jnp.int32),
            pltpu.VMEM((batches, choose, toks), BF16),
            pltpu.VMEM((units, total_rows), BF16),
            pltpu.VMEM((units, features), BF16),
            dma((5 + batches,)),
            pltpu.VMEM((batches, window * cap, toks), BF16),
            pltpu.VMEM((nz, window, batches, cap, cw), BF16),
            pltpu.VMEM((window, batches, cap, 128), BF16),
            pltpu.VMEM((nz, batches, RING, 2, cap, cw), BF16),
            pltpu.VMEM((batches, RING, 2, cap, 128), BF16),
            pltpu.VMEM((total_rows, 128), F32),
            pltpu.VMEM((8, total_rows), F32),
            pltpu.VMEM((units, total_rows), F32),
            pltpu.VMEM((total_rows, 128), F32),
            pltpu.VMEM((nz, nx, depth, 128), BF16),
            pltpu.VMEM((nz, nx - 1, depth, 128), BF16),
            pltpu.VMEM((nz, depth, 128), F32),
            pltpu.VMEM((nz - 1, depth, 128), F32),
            pltpu.VMEM((nz, nx, half, 128), BF16),
            pltpu.VMEM((nz - 1, nx, half, 128), BF16),
            pltpu.VMEM((nx, half, 128), F32),
            pltpu.VMEM((nx - 1, half, 128), F32),
            pltpu.VMEM((2, 8, 128), F32),
            pltpu.VMEM((nx - 1, 8, 128), F32),
            pltpu.VMEM((nz - 1, 8, 128), F32),
            pltpu.VMEM((peers, 1, 128), F32),
            pltpu.VMEM((peers - 1, 1, 128), F32),
            dma((nz + 1, 3)), dma((nz + 1, 3)), dma((nz + 1, 4)), dma((nz + 1, 4)),
            dma((nz + 1,)), dma((nz + 1,)), dma((nz,)), dma((nz,)),
            dma((nz,)), dma((nz,)), dma((nz,)), dma((nz,)), dma, dma, dma((2,)), dma((2,)), dma, dma,
        ],
        compiler_params=pltpu.CompilerParams(
            collective_id=0, has_side_effects=True, vmem_limit_bytes=60 * 1024 * 1024
        ),
    )(
        d_out,
        jnp.swapaxes(routes, 1, 2),
        jnp.swapaxes(slots, 1, 2),
        jnp.swapaxes(route_probs, 1, 2),
        jnp.swapaxes(token_counts, 0, 1),
        jnp.swapaxes(hidden[:, 0], 1, 2),
        w_down,
    )
    return jnp.swapaxes(dh, 1, 2)[:, None], dw, jnp.swapaxes(dp, 1, 2)


def solution(mesh):
    nx = math.isqrt(mesh.shape["dp"])
    nz = mesh.shape["dp"] // nx
    both = ("dp", "expert")
    in_specs = (
        P(None, both, None),
        P(None, both, None),
        P(None, both, None),
        P(None, both, None),
        P(None, both),
        P(None, "dp", None, "expert"),
        P("expert", None),
    )
    out_specs = (P(None, "dp", None, "expert"), P("dp", "expert"), P(None, both, None))
    return jax.shard_map(
        functools.partial(on_device, nz, nx), mesh=mesh, in_specs=in_specs, out_specs=out_specs, check_vma=False
    )
```
